32 devices in a mesh: space: 16 (over z, y, x), sample: 2 (over core).
Axes of the slice: x: 2, y: 2, z: 4, core: 2. Of those that a mesh axis runs over, the one named last changes fastest.
Arguments:
- features: bfloat16 [2, 16, 1, 8, 8, 768], P('sample', 'space'), may hold values from -12 to 12
- wall_mask: int32 [2, 16, 1, 8, 64], P('sample', 'space'), may hold values 0 or 1
- block_positions: int32 [2, 16, 1], P('sample'), may hold values from -1 to 3, as said below
- dw_kernel: float32 [5, 5, 5, 96], replicated, may hold values from -0.5 to 0.5
- norm_gain: float32 [96], replicated, may hold values from 0.1 to 1.9
- norm_bias: float32 [96], replicated, may hold values from -3 to 3
- w_in: bfloat16 [96, 384], replicated, may hold values from -0.625 to 0.625
- b_in: float32 [384], replicated, may hold values from -3 to 3
- w_out: bfloat16 [384, 96], replicated, may hold values from -0.3125 to 0.3125
- b_out: float32 [96], replicated, may hold values from -3 to 3
- layer_scale: float32 [96], replicated, may hold values from 0.3 to 1.5
- upstream: bfloat16 [2, 16, 1, 8, 8, 768], P('sample', 'space'), may hold values from -6 to 6
Outputs:
- mixed: bfloat16 [2, 16, 1, 8, 8, 768], P('sample', 'space')
- grad_features: bfloat16 [2, 16, 1, 8, 8, 768], P('sample', 'space')
- grad_kernel: float32 [5, 5, 5, 96], replicated
- grad_w_in: float32 [96, 384], replicated
- grad_w_out: float32 [384, 96], replicated
- grad_b_in: float32 [384], replicated
- grad_vectors: float32 [4, 96], replicated
The draws below stay inside these ranges and needn't reach their ends.
Inputs may be any that keep to these rules, and one draw needn't show every extreme that they name: `block_positions`: in each layer the live slots come first and hold distinct positions; each layer holds exactly 1 block, in slot 0; the first layer of every sample is full and holds position 3.
All inputs are finite; a program needn't handle non-finite values. No bound on the sum of `wall_mask` on one device may be relied on, other than what follows from the above.
Results may differ from the reference program's by a relative error of at most 0.007.
Values may be sent and summed in bfloat16 or wider, within the bound.
No kernel may reach another device: no remote copies, remote signals or barrier semaphores. Data moves between devices by JAX's collectives and lax.ppermute only.
A program may use at most 64 MiB of HBM per device.

```python
import math
import jax
import jax.numpy as jnp
from jax import lax

C = 96
HID = 384
BLOCK = 8
KS = 5
SLOTS = 1
GRID = 2
LAYERS = 16
SAMPLES = 2
VOXELS = 16384


def draw_features(key, part):
    key = jax.random.fold_in(key, 11)
    key_values, key_voxel, key_channel = jax.random.split(key, 3)
    full_shape = (SAMPLES, LAYERS, SLOTS, BLOCK, BLOCK, BLOCK, C)
    voxel_shape = (SAMPLES, LAYERS, SLOTS, BLOCK, BLOCK, BLOCK, 1)
    values = jax.random.normal(key_values, full_shape, jnp.float32)
    voxel_scale = jnp.exp(jax.random.uniform(key_voxel, voxel_shape, jnp.float32, math.log(0.3), math.log(3.0)))
    channel_scale = jnp.exp(jax.random.uniform(key_channel, (C,), jnp.float32, math.log(0.5), math.log(2.0)))
    field = jnp.clip(values * voxel_scale * channel_scale, -12.0, 12.0)
    return field.reshape(SAMPLES, LAYERS, SLOTS, BLOCK, BLOCK, BLOCK * C).astype(jnp.bfloat16)


def draw_block_positions(key, part):
    key = jax.random.fold_in(key, 23)
    key_order, key_count = jax.random.split(key)
    cell_count = GRID * GRID
    scores = jax.random.randint(key_order, (SAMPLES, LAYERS, cell_count), 0, 1 << 20) * cell_count + jnp.arange(cell_count, dtype=jnp.int32)
    first_layer = jnp.arange(LAYERS, dtype=jnp.int32)[None, :, None] == 0
    last_cell = jnp.arange(cell_count, dtype=jnp.int32)[None, None, :] == cell_count - 1
    scores = jnp.where(first_layer & last_cell, -1, scores)
    cell_order = jnp.argsort(scores, axis=-1, stable=True)[..., :SLOTS].astype(jnp.int32)
    counts = jax.random.randint(key_count, (SAMPLES, LAYERS, 1), 1, SLOTS + 1)
    counts = jnp.where(first_layer, SLOTS, counts)
    slot_ids = jnp.arange(SLOTS, dtype=jnp.int32)[None, None, :]
    return jnp.where(slot_ids < counts, cell_order, -1).astype(jnp.int32)


def plant(result, rng, low, top_value):
    longest = result.shape.index(max(result.shape))
    spots = []
    for shift in (0, 1):
        where = [jax.random.randint(jax.random.fold_in(rng, axis), (), 0, length) for axis, length in enumerate(result.shape)]
        where[longest] = (where[longest] + shift) % result.shape[longest]
        spots.append(tuple(where))
    return result.at[spots[0]].set(low).at[spots[1]].set(top_value)


def levels(stream_key, dims, shards, least, top_value):
    level = 1.0
    for dim, shards_of in shards:
        heights = jax.random.uniform(jax.random.fold_in(jax.random.fold_in(stream_key, 6), dim), (shards_of,), jnp.float32, least / len(shards), top_value / len(shards))
        level = level * jnp.repeat(jnp.exp(heights), dims[dim] // shards_of).reshape((-1,) + (1,) * (len(dims) - 1 - dim))
    return level


def scatter_about(rng, extent, deviation, bound, shards=(), held_as=jnp.bfloat16):
    result = deviation * jax.random.normal(rng, extent, jnp.float32)
    if shards:
        result = result * levels(rng, extent, shards, -0.22, 0.18)
    return jnp.clip(result, -bound, bound).astype(held_as)


def setup_inputs(seed: int = 0) -> dict:
    streams_of = jax.random.split(jax.random.key(seed), 13)
    return {
        "features": draw_features(jax.random.fold_in(streams_of[12], 71), 0),
        "wall_mask": plant((jax.random.randint(streams_of[1], (SAMPLES, LAYERS, SLOTS, BLOCK, BLOCK * BLOCK), 0, 4) < 1).astype(jnp.int32), jax.random.fold_in(streams_of[1], 1), 0, 1),
        "block_positions": draw_block_positions(jax.random.fold_in(streams_of[12], 71), 0),
        "dw_kernel": scatter_about(streams_of[3], (KS, KS, KS, C), (KS * KS * KS) ** -0.5, 0.5, (), jnp.float32),
        "norm_gain": jnp.clip(1.0 + 0.18 * jax.random.normal(streams_of[4], (C,), jnp.float32), 0.1, 1.9),
        "norm_bias": scatter_about(streams_of[5], (C,), 0.5, 3.0, (), jnp.float32),
        "w_in": scatter_about(streams_of[6], (C, HID), C ** -0.5, 0.625),
        "b_in": scatter_about(streams_of[7], (HID,), 0.5, 3.0, (), jnp.float32),
        "w_out": scatter_about(streams_of[8], (HID, C), HID ** -0.5, 0.3125),
        "b_out": scatter_about(streams_of[9], (C,), 0.5, 3.0, (), jnp.float32),
        "layer_scale": jnp.clip(jnp.exp(jax.random.uniform(streams_of[10], (C,), jnp.float32, math.log(0.3), math.log(1.5))), 0.3, 1.5),
        "upstream": scatter_about(streams_of[11], (SAMPLES, LAYERS, SLOTS, BLOCK, BLOCK, BLOCK * C), 1.0, 6.0, ((0, 2), (1, 16))),
    }


GELU_SCALE = 0.7978845608028654
GELU_CUBIC = 0.044715
NORM_EPS = 1e-06

def gelu_value(pre_act):
    inner = GELU_SCALE * (pre_act + GELU_CUBIC * pre_act * pre_act * pre_act)
    return 0.5 * pre_act * (1.0 + jnp.tanh(inner))

def gelu_slope(pre_act):
    inner = GELU_SCALE * (pre_act + GELU_CUBIC * pre_act * pre_act * pre_act)
    tanh_value = jnp.tanh(inner)
    return 0.5 * (1.0 + tanh_value) + 0.5 * pre_act * (1.0 - tanh_value * tanh_value) * GELU_SCALE * (1.0 + 3.0 * GELU_CUBIC * pre_act * pre_act)

def expand_fluid(wall_rows, channels):
    block_edge = wall_rows.shape[-2]
    lead_shape = wall_rows.shape[:-2]
    fluid_mask = (1 - wall_rows).astype(jnp.bfloat16).reshape(lead_shape + (block_edge, block_edge, block_edge, 1))
    fluid_mask = jnp.broadcast_to(fluid_mask, lead_shape + (block_edge, block_edge, block_edge, channels))
    return fluid_mask.reshape(lead_shape + (block_edge, block_edge, block_edge * channels))

def edge_range(step_now, block_edge):
    if step_now < 0:
        return (block_edge - 2, block_edge)
    if step_now > 0:
        return (0, 2)
    return (0, block_edge)

def select_blocks(source, own_pos, source_pos, step_y, step_x, grid_side):
    own_y = own_pos // grid_side
    own_x = own_pos % grid_side
    target_y = own_y + step_y
    target_x = own_x + step_x
    inside = (own_pos >= 0) & (target_y >= 0) & (target_y < grid_side) & (target_x >= 0) & (target_x < grid_side)
    target = target_y * grid_side + target_x
    match = (source_pos[None, :] == target[:, None]) & inside[:, None] & (source_pos[None, :] >= 0)
    chosen = jnp.where(match[:, :, None, None, None], source[None], jnp.zeros((), source.dtype))
    return lax.optimization_barrier(jnp.sum(chosen, axis=1)).astype(source.dtype)

def assemble(own_field, below_rims, above_rims, own_pos, below_pos, above_pos, grid_side):
    block_edge = own_field.shape[1]
    channels = own_field.shape[3] // block_edge
    row_parts = []
    for step_y in (-1, 0, 1):
        col_parts = []
        for step_x in (-1, 0, 1):
            y_low, y_high = edge_range(step_y, block_edge)
            x_low, x_high = edge_range(step_x, block_edge)
            pieces = []
            for source, source_pos in ((below_rims, below_pos), (own_field, own_pos), (above_rims, above_pos)):
                trimmed = source[:, :, y_low:y_high, x_low * channels:x_high * channels]
                pieces.append(select_blocks(trimmed, own_pos, source_pos, step_y, step_x, grid_side))
            col_parts.append(jnp.concatenate(pieces, axis=1))
        row_parts.append(jnp.concatenate(col_parts, axis=3))
    return jnp.concatenate(row_parts, axis=2)

def depthwise(padded, dw_kernel, block_edge):
    channels = dw_kernel.shape[3]
    tap_count = dw_kernel.shape[0]
    running = jnp.zeros((padded.shape[0], block_edge, block_edge, block_edge * channels), jnp.float32)
    for tap_z in range(tap_count):
        for tap_y in range(tap_count):
            for tap_x in range(tap_count):
                weight_row = jnp.tile(dw_kernel[tap_z, tap_y, tap_x], block_edge)
                window = padded[:, tap_z:tap_z + block_edge, tap_y:tap_y + block_edge, tap_x * channels:(tap_x + block_edge) * channels]
                running = running + window.astype(jnp.float32) * weight_row
    return running

def kernel_grad(padded, grad_conv, block_edge, tap_count):
    channels = padded.shape[3] // (block_edge + tap_count - 1)
    grad_wide = grad_conv.astype(jnp.float32)
    rows_list = []
    for tap_z in range(tap_count):
        for tap_y in range(tap_count):
            for tap_x in range(tap_count):
                window = padded[:, tap_z:tap_z + block_edge, tap_y:tap_y + block_edge, tap_x * channels:(tap_x + block_edge) * channels]
                per_lane = lax.optimization_barrier(jnp.sum(window.astype(jnp.float32) * grad_wide, axis=(0, 1, 2)))
                rows_list.append(lax.optimization_barrier(jnp.sum(per_lane.reshape(block_edge, channels), axis=0)))
    return jnp.stack(rows_list).reshape(tap_count, tap_count, tap_count, channels)

def dense_step(conv_slot, field_slot, live_value, upstream_slot, norm_gain, norm_bias, w_in, b_in, w_out, b_out, layer_scale):
    channels = norm_gain.shape[0]
    slot_shape = field_slot.shape
    conv_rows = conv_slot.reshape(-1, channels)
    row_mean = lax.optimization_barrier(jnp.mean(conv_rows, axis=1, keepdims=True))
    centred = conv_rows - row_mean
    row_var = lax.optimization_barrier(jnp.mean(centred * centred, axis=1, keepdims=True))
    inv_std = lax.rsqrt(row_var + NORM_EPS)
    unit_rows = centred * inv_std
    normed = (unit_rows * norm_gain + norm_bias).astype(jnp.bfloat16)
    pre_act = jnp.dot(normed, w_in, preferred_element_type=jnp.float32) + b_in
    activated = gelu_value(pre_act).astype(jnp.bfloat16)
    branch = jnp.dot(activated, w_out, preferred_element_type=jnp.float32) + b_out
    field_rows = field_slot.reshape(-1, channels).astype(jnp.float32)
    mixed = ((field_rows + layer_scale * branch) * live_value).astype(jnp.bfloat16)
    seed_grad = upstream_slot.reshape(-1, channels).astype(jnp.float32) * live_value
    scale_grad = lax.optimization_barrier(jnp.sum(seed_grad * branch, axis=0))
    grad_branch = (seed_grad * layer_scale).astype(jnp.bfloat16)
    bout_grad = lax.optimization_barrier(jnp.sum(grad_branch.astype(jnp.float32), axis=0))
    wout_grad = jnp.dot(activated.T, grad_branch, preferred_element_type=jnp.float32)
    grad_act = jnp.dot(grad_branch, w_out.T, preferred_element_type=jnp.float32)
    grad_pre = (grad_act * gelu_slope(pre_act)).astype(jnp.bfloat16)
    bin_grad = lax.optimization_barrier(jnp.sum(grad_pre.astype(jnp.float32), axis=0))
    win_grad = jnp.dot(normed.T, grad_pre, preferred_element_type=jnp.float32)
    grad_normed = jnp.dot(grad_pre, w_in.T, preferred_element_type=jnp.float32)
    gain_grad = lax.optimization_barrier(jnp.sum(grad_normed * unit_rows, axis=0))
    bias_grad = lax.optimization_barrier(jnp.sum(grad_normed, axis=0))
    scaled = grad_normed * norm_gain
    grad_conv = inv_std * (scaled - lax.optimization_barrier(jnp.mean(scaled, axis=1, keepdims=True)) - unit_rows * lax.optimization_barrier(jnp.mean(scaled * unit_rows, axis=1, keepdims=True)))
    grad_conv = grad_conv.astype(jnp.bfloat16).reshape(slot_shape)
    vectors = jnp.stack([gain_grad, bias_grad, bout_grad, scale_grad])
    return (mixed.reshape(slot_shape), grad_conv, (win_grad, wout_grad, bin_grad, vectors))

def neighbours(field, positions, block_edge):
    rims_below = jnp.concatenate([jnp.zeros_like(field[:1, :, block_edge - 2:]), field[:-1, :, block_edge - 2:]], axis=0)
    rims_above = jnp.concatenate([field[1:, :, :2], jnp.zeros_like(field[:1, :, :2])], axis=0)
    empty_row = jnp.full(positions[:1].shape, -1, jnp.int32)
    below_pos = jnp.concatenate([empty_row, positions[:-1]], axis=0)
    above_pos = jnp.concatenate([positions[1:], empty_row], axis=0)
    return (rims_below, rims_above, below_pos, above_pos)

def reference(features, wall_mask, block_positions, dw_kernel, norm_gain, norm_bias, w_in, b_in, w_out, b_out, layer_scale, upstream):
    channels = dw_kernel.shape[3]
    tap_count = dw_kernel.shape[0]
    block_edge = features.shape[3]
    hidden_units = w_in.shape[1]
    flipped = dw_kernel[::-1, ::-1, ::-1]
    start = (jnp.zeros(dw_kernel.shape, jnp.float32), jnp.zeros(w_in.shape, jnp.float32), jnp.zeros(w_out.shape, jnp.float32), jnp.zeros((hidden_units,), jnp.float32), jnp.zeros((4, channels), jnp.float32))

    def slot_step(slot_items):
        return dense_step(slot_items[0], slot_items[1], slot_items[2], slot_items[3], norm_gain, norm_bias, w_in, b_in, w_out, b_out, layer_scale)

    def one_sample(sums, sample_items):
        sample_field, sample_walls, positions, sample_up = sample_items
        live_flag = (positions >= 0).astype(jnp.bfloat16)
        fluid_mask = expand_fluid(sample_walls, channels)
        masked = sample_field * fluid_mask * live_flag[:, :, None, None, None]
        rims_below, rims_above, below_pos, above_pos = neighbours(masked, positions, block_edge)

        def first_pass(carried, layer_items):
            own_field, below_rims, above_rims, own_pos, low_pos, high_pos, field_layer, up_layer, live_layer = layer_items
            padded = assemble(own_field, below_rims, above_rims, own_pos, low_pos, high_pos, GRID)
            conv_out = depthwise(padded, dw_kernel, block_edge)
            mixed_layer, grad_conv, grads = lax.map(slot_step, (conv_out, field_layer, live_layer.astype(jnp.float32), up_layer))
            kernel_term = kernel_grad(padded, grad_conv, block_edge, tap_count)
            carried = (carried[0] + kernel_term, carried[1] + lax.optimization_barrier(jnp.sum(grads[0], axis=0)), carried[2] + lax.optimization_barrier(jnp.sum(grads[1], axis=0)), carried[3] + lax.optimization_barrier(jnp.sum(grads[2], axis=0)), carried[4] + lax.optimization_barrier(jnp.sum(grads[3], axis=0)))
            return (carried, (mixed_layer, grad_conv))
        sums, (mixed_sample, grad_conv_all) = lax.scan(first_pass, sums, (masked, rims_below, rims_above, positions, below_pos, above_pos, sample_field, sample_up, live_flag))
        grad_below, grad_above, below_again, above_again = neighbours(grad_conv_all, positions, block_edge)

        def second_pass(unused, layer_items):
            own_grad, below_grad, above_grad, own_pos, low_pos, high_pos, fluid_layer, up_layer, live_layer = layer_items
            grad_padded = assemble(own_grad, below_grad, above_grad, own_pos, low_pos, high_pos, GRID)
            back_conv = depthwise(grad_padded, flipped, block_edge)
            live_wide = live_layer.astype(jnp.float32)[:, None, None, None]
            seed_grad = up_layer.astype(jnp.float32) * live_wide
            return (unused, (seed_grad + back_conv * fluid_layer * live_wide).astype(jnp.bfloat16))
        unused_out, grad_sample = lax.scan(second_pass, jnp.zeros((), jnp.float32), (grad_conv_all, grad_below, grad_above, positions, below_again, above_again, fluid_mask, sample_up, live_flag))
        return (sums, (mixed_sample, grad_sample))
    sums, (mixed, grad_features) = lax.scan(one_sample, start, (features, wall_mask, block_positions, upstream))
    factor = 1.0 / math.sqrt(VOXELS)
    return (mixed, grad_features, sums[0] * factor, sums[1] * factor, sums[2] * factor, sums[3] * factor, sums[4] * factor)
```

```python
import functools
import math

import jax
import jax.numpy as jnp
from jax import lax
from jax.experimental import pallas as pl
from jax.experimental.pallas import tpu as pltpu
from jax.sharding import PartitionSpec as P

GELU_SCALE = 0.7978845608028654
GELU_CUBIC = 0.044715
NORM_EPS = 1e-06

B = 8
T = 5
C = 96
HID = 384
LANES = 128

ROW_IN = 0
ROW_OUT = 288
ROW_KERNEL = 576
ROW_BIN = 704
ROW_VEC = 707
ROWS = 712

F32 = jnp.float32
BF16 = jnp.bfloat16

VMEM_LIMIT = 48 * 1024 * 1024


def params():
    return pltpu.CompilerParams(vmem_limit_bytes=VMEM_LIMIT)


def vmem():
    return pl.BlockSpec(memory_space=pltpu.VMEM)


def hbm():
    return pl.BlockSpec(memory_space=pltpu.HBM)


def pinned(array):
    return pltpu.with_memory_space_constraint(array, pltpu.HBM)


def start_copies(sems, *pairs):
    copies = [
        pltpu.make_async_copy(source, target, sems.at[k])
        for k, (source, target) in enumerate(pairs)
    ]
    for copy in copies:
        copy.start()
    return copies


def layer_places(table_ref):
    layer = lax.axis_index("space")
    count = lax.axis_size("space")
    own = table_ref[layer]
    low = table_ref[jnp.maximum(layer - 1, 0)]
    high = table_ref[jnp.minimum(layer + 1, count - 1)]
    live = jnp.where(own >= 0, 1.0, 0.0).astype(F32)
    return jnp.maximum(own, 0), jnp.maximum(low, 0), jnp.maximum(high, 0), live


def is_even():
    return (lax.axis_index("space") & 1) == 0


def halo_planes(even_ref, odd_ref):
    even = is_even()

    def low(k):
        return jnp.where(even, odd_ref[k].astype(F32), even_ref[k].astype(F32))

    def high(k):
        return jnp.where(even, even_ref[k].astype(F32), odd_ref[k].astype(F32))

    return low, high


def offset(own, other):
    dy = (other >> 1) - (own >> 1)
    dx = (other & 1) - (own & 1)
    return 8 * dx, 8 * dy


def spread(field):
    return [field[:, x * C : (x + 1) * C] for x in range(B)]


def gather_lanes(parts):
    return jnp.concatenate(parts, axis=-1)


def send_kernel(
    table_hbm,
    feat_hbm,
    wall_hbm,
    up_hbm,
    dw_hbm,
    even_ref,
    odd_ref,
    masked_ref,
    fluid_ref,
    dw_ref,
    table_ref,
    feat_ref,
    wall_ref,
    up_ref,
    sems,
):
    copies = start_copies(
        sems,
        (wall_hbm, wall_ref),
        (feat_hbm, feat_ref),
        (up_hbm, up_ref),
        (table_hbm, table_ref),
        (dw_hbm, dw_ref),
    )
    copies[3].wait()
    _, _, _, live = layer_places(table_ref)
    copies[0].wait()
    walls = wall_ref[...]
    fluid = (1 - walls).astype(F32)
    row = lax.broadcasted_iota(jnp.int32, (B, B * B), 0)
    lane = lax.broadcasted_iota(jnp.int32, (B, B * B), 1)
    pick = (lane >> 3) == row
    tall = jnp.concatenate(
        [jnp.where(pick, fluid[z : z + 1, :], 0.0) for z in range(B)], axis=0
    ).astype(BF16)
    src = lax.broadcasted_iota(jnp.int32, (B * B, B * C), 0) & 7
    dst = lax.broadcasted_iota(jnp.int32, (B * B, B * C), 1)
    widen = jnp.where((dst >= src * C) & (dst < src * C + C), 1.0, 0.0).astype(BF16)
    wide = jnp.dot(tall, widen, preferred_element_type=F32)
    copies[1].wait()
    copies[2].wait()
    for z in range(B):
        fluid_z = wide[z * B : (z + 1) * B, :]
        fluid_ref[z] = fluid_z.astype(BF16)
        masked = (feat_ref[z].astype(F32) * (fluid_z * live)).astype(BF16)
        masked_ref[z] = masked

    def payload(target, first):
        target[0:4] = masked_ref[first : first + 4]
        for k in range(2):
            plane = k if first == 0 else 6 + k
            target[4 + k] = (up_ref[plane].astype(F32) * live).astype(BF16)

    @pl.when(is_even())
    def _():
        payload(even_ref, 4)
        payload(odd_ref, 0)

    @pl.when(jnp.logical_not(is_even()))
    def _():
        payload(even_ref, 0)
        payload(odd_ref, 4)

    copies[4].wait()


def wide_taps(dw_ref, taps):
    for a in range(T):
        for b in range(T):
            for e in range(T):
                taps[a, b, e] = jnp.broadcast_to(dw_ref[a, b, e : e + 1, :], (B, C))


class Flipped:
    def __init__(self, taps):
        self.taps = taps

    def __getitem__(self, index):
        a, b, e = index
        return self.taps[T - 1 - a, T - 1 - b, T - 1 - e]


def rows_of():
    return lax.broadcasted_iota(jnp.int32, (B, C), 0)


def put_halo(halo, plane, parts, start):
    for x in range(B):
        halo[plane, start + 10 + x] = parts[x]


def clear_halo(halo, planes):
    for p in range(planes):
        halo[p, 8:20] = jnp.zeros((12, B, C), F32)


def add_own(acc, window, taps, a, b):
    for e in range(T):
        weight = taps[a, b, e]
        for x in range(B):
            if 0 <= x + e - 2 < B:
                acc[x] = acc[x] + window[x + e - 2] * weight


def add_halo(acc, window, taps, a, b):
    for e in range(T):
        weight = taps[a, b, e]
        for x in range(B):
            acc[x] = acc[x] + window[x + e] * weight


def row_masks(start=None):
    masks = []
    for by in range(-2, 3):
        row = rows_of() + by if start is None else rows_of() + (by - start)
        inside = (row >= 0) & (row < B)
        masks.append(None if start is None and by == 0 else jnp.where(inside, 1.0, 0.0))
    return masks


def shift_rows(value, by, masks):
    rolled = value if by == 0 else pltpu.roll(value, (-by) % B, 0)
    mask = masks[by + 2]
    return rolled if mask is None else rolled * mask


def conv_plane(source, taps, own, masks, halo=None, halos=(), halo_masks=None):
    out = [jnp.zeros((B, C), F32) for _ in range(B)]
    for b in range(T):
        if own:
            acc = [jnp.zeros((B, C), F32) for _ in range(B)]
            for a, plane in own:
                add_own(acc, [source[plane, x] for x in range(B)], taps, a, b)
            for x in range(B):
                out[x] = out[x] + shift_rows(acc[x], b - 2, masks)
        if halos:
            acc = [jnp.zeros((B, C), F32) for _ in range(B)]
            for a, plane in halos:
                add_halo(acc, [halo[plane, 8 + j] for j in range(12)], taps, a, b)
            for x in range(B):
                out[x] = out[x] + shift_rows(acc[x], b - 2, halo_masks)
    return out


def middle_plane(source, taps, first, masks):
    return conv_plane(source, taps, [(a, first + a) for a in range(T)], masks)


OWN_TAPS = {0: (2, 3, 4), 1: (1, 2, 3, 4), 6: (0, 1, 2, 3), 7: (0, 1, 2)}


def own_pairs(plane):
    return [(a, plane + a - 2) for a in OWN_TAPS.get(plane, range(T))]


def dense_weights(refs):
    gain, bias, w_in, b_in, w_out, b_out, scale = refs
    b_out = None if b_out is None else b_out[...]
    return (
        gain[...],
        bias[...],
        w_in[...],
        b_in[...].reshape(1, HID),
        w_out[...],
        b_out,
        scale[...],
    )


def dense_part(conv_rows, seed, weights, own=True):
    gain, bias, w_in, b_in, w_out_t, b_out, scale = weights
    mean = jnp.sum(conv_rows, axis=1, keepdims=True) * (1.0 / C)
    centred = conv_rows - mean
    var = jnp.sum(centred * centred, axis=1, keepdims=True) * (1.0 / C)
    inv_std = lax.rsqrt(var + NORM_EPS)
    unit = centred * inv_std
    normed = (unit * gain + bias).astype(BF16)
    pre = jnp.dot(normed, w_in, preferred_element_type=F32) + b_in
    square = pre * pre
    inner = pre * (GELU_SCALE + (GELU_SCALE * GELU_CUBIC) * square)
    tanh = jnp.tanh(inner)
    half = 0.5 + 0.5 * tanh
    slope = half + (0.5 * pre) * (1.0 - tanh * tanh) * (
        GELU_SCALE + (3.0 * GELU_SCALE * GELU_CUBIC) * square
    )
    grad_branch = (seed * scale).astype(BF16)
    grad_act = jnp.dot(grad_branch, w_out_t, preferred_element_type=F32)
    grad_pre = (grad_act * slope).astype(BF16)
    grad_normed = lax.dot_general(
        grad_pre, w_in, (((1,), (1,)), ((), ())), preferred_element_type=F32
    )
    scaled = grad_normed * gain
    mean_s = jnp.sum(scaled, axis=1, keepdims=True) * (1.0 / C)
    mean_su = jnp.sum(scaled * unit, axis=1, keepdims=True) * (1.0 / C)
    grad_conv = inv_std * (scaled - mean_s - unit * mean_su)
    grad_conv = grad_conv.astype(BF16).astype(F32).reshape(-1, B, B, C)
    if not own:
        return grad_conv
    activated = (pre * half).astype(BF16)
    branch = (
        lax.dot_general(activated, w_out_t, (((1,), (1,)), ((), ())), preferred_element_type=F32)
        + b_out
    )
    grad_in = lax.dot_general(
        normed, grad_pre, (((0,), (0,)), ((), ())), preferred_element_type=F32
    )
    grad_out = lax.dot_general(
        grad_branch, activated, (((0,), (0,)), ((), ())), preferred_element_type=F32
    )
    vec = jnp.concatenate(
        [
            jnp.sum(grad_normed * unit, axis=0, keepdims=True),
            jnp.sum(grad_normed, axis=0, keepdims=True),
            jnp.sum(grad_branch.astype(F32), axis=0, keepdims=True),
            jnp.sum(seed * branch, axis=0, keepdims=True),
        ],
        axis=0,
    )
    bin_sum = jnp.sum(grad_pre.astype(F32), axis=0, keepdims=True)
    return grad_conv, branch.reshape(-1, B, B, C), grad_in, grad_out, vec, bin_sum


def kernel_taps(pairs):
    acc = [[jnp.zeros((B, C), F32) for _ in range(2)] for _ in range(T)]
    for grads, window, inside in pairs:
        for e in range(T):
            for x in range(B):
                if inside:
                    if not 0 <= x + e - 2 < B:
                        continue
                    value = window[x + e - 2]
                else:
                    value = window[x + e]
                acc[e][x & 1] = acc[e][x & 1] + value * grads[x]
    return [pair[0] + pair[1] for pair in acc]


def move_rows(grads, moved, k, masks):
    for x in range(B):
        for b in range(T):
            moved[b, k, x] = shift_rows(grads[x], 2 - b, masks)


def early_kernel(
    masked_ref,
    dw_ref,
    table_hbm,
    up_hbm,
    gain_hbm,
    bias_hbm,
    w_in_hbm,
    b_in_hbm,
    w_out_hbm,
    b_out_hbm,
    scale_hbm,
    source,
    seeds,
    taps,
    conv,
    gain_ref,
    bias_ref,
    w_in_ref,
    b_in_ref,
    w_out_ref,
    b_out_ref,
    scale_ref,
    gc_ref,
    branch_ref,
    grad_in_ref,
    grad_out_ref,
    vec_ref,
    bin_ref,
    rows_ref,
    table_vmem,
    table_ref,
    up_ref,
    moved,
    sems,
):
    copies = start_copies(
        sems,
        (table_hbm, table_ref),
        (up_hbm, up_ref),
        (gain_hbm, gain_ref),
        (bias_hbm, bias_ref),
        (w_in_hbm, w_in_ref),
        (b_in_hbm, b_in_ref),
        (w_out_hbm, w_out_ref),
        (b_out_hbm, b_out_ref),
        (scale_hbm, scale_ref),
        (table_hbm, table_vmem),
    )

    def own_planes(z, carry):
        field = spread(masked_ref[z].astype(F32))
        for x in range(B):
            source[z, x] = field[x]
        return carry

    lax.fori_loop(0, B, own_planes, 0, unroll=True)
    wide_taps(dw_ref, taps)
    masks = row_masks()

    def middle_step(z, carry):
        out = middle_plane(source, taps, z, masks)
        for x in range(B):
            conv[2 + z, x] = out[x]
        return carry

    lax.fori_loop(0, 4, middle_step, 0)

    def edge(plane):
        out = conv_plane(source, taps, own_pairs(plane), masks)
        for x in range(B):
            conv[plane, x] = out[x]

    for plane in (0, 1, 6, 7):
        edge(plane)
    for copy in copies:
        copy.wait()
    live = layer_places(table_ref)[3]

    def own_seeds(z, carry):
        seed = spread(up_ref[z].astype(F32) * live)
        for x in range(B):
            seeds[z, x] = seed[x]
        return carry

    lax.fori_loop(0, B, own_seeds, 0, unroll=True)
    refs = (gain_ref, bias_ref, w_in_ref, b_in_ref, w_out_ref, b_out_ref, scale_ref)
    grad_conv, branch, grad_in, grad_out, vec, bin_sum = dense_part(
        conv[2:6].reshape(256, C), seeds[2:6].reshape(256, C), dense_weights(refs)
    )
    gc_ref[...] = grad_conv
    branch_ref[...] = branch
    grad_in_ref[...] = grad_in
    grad_out_ref[...] = grad_out
    vec_ref[...] = vec
    bin_ref[...] = bin_sum

    for k in range(4):
        move_rows([gc_ref[k, x] for x in range(B)], moved, k, masks)

    def kernel_step(b, carry):
        for a in range(T):
            sums = kernel_taps(
                (
                    [moved[b, k, x] for x in range(B)],
                    [source[k + a, x] for x in range(B)],
                    True,
                )
                for k in range(4)
            )
            for e in range(T):
                rows_ref[a * T + b, e] = sums[e]
        return carry

    lax.fori_loop(0, T, kernel_step, 0)


NEAR = {0: [(0, 0), (1, 1)], 1: [(0, 1)], 6: [(4, 2)], 7: [(3, 2), (4, 3)]}


def main_kernel(
    chunk,
    parts,
    odd_ref,
    even_ref,
    source,
    seeds,
    taps,
    conv_ref,
    gain_ref,
    bias_ref,
    w_in_ref,
    b_in_ref,
    w_out_ref,
    b_out_ref,
    scale_ref,
    early_gc,
    early_branch,
    early_in,
    early_out,
    early_vec,
    early_bin,
    early_rows,
    table_vmem,
    branch_ref,
    gc_ref,
    packed_ref,
    table_ref,
    sems,
    halo,
    conv,
    moved,
    moved_halo,
    kernel_rows,
    pack,
):
    copies = start_copies(sems, (table_vmem, table_ref))
    clear_halo(halo, 4)
    pack[ROW_KERNEL:ROWS, :] = jnp.zeros((ROWS - ROW_KERNEL, LANES), F32)
    gc_ref[2:6] = early_gc[...]
    branch_ref[2:6] = early_branch[...]

    from_low, from_high = halo_planes(even_ref, odd_ref)
    below = [spread(from_low(2 + k)) for k in range(2)]
    above = [spread(from_high(k)) for k in range(2)]
    copies[0].wait()
    own, low, high, _ = layer_places(table_ref)
    low_x, low_y = offset(own, low)
    high_x, high_y = offset(own, high)
    for k in range(2):
        put_halo(halo, k, below[k], low_x)
        put_halo(halo, 2 + k, above[k], high_x)
    low_masks, high_masks = row_masks(low_y), row_masks(high_y)
    for k, plane in enumerate((0, 1, 6, 7)):
        near = low_masks if k < 2 else high_masks
        out = conv_plane(source, taps, [], None, halo, NEAR[plane], near)
        for x in range(B):
            conv[k, x] = conv_ref[plane, x] + out[x]

    late = jnp.concatenate([seeds[0:2], seeds[6:8]], axis=0)
    refs = (gain_ref, bias_ref, w_in_ref, b_in_ref, w_out_ref, b_out_ref, scale_ref)
    grad_conv, branch, grad_in, grad_out, vec, bin_sum = dense_part(
        conv[...].reshape(256, C), late.reshape(256, C), dense_weights(refs)
    )
    gc_ref[0:2] = grad_conv[0:2]
    gc_ref[6:8] = grad_conv[2:4]
    branch_ref[0:2] = branch[0:2]
    branch_ref[6:8] = branch[2:4]
    pack[ROW_VEC : ROW_VEC + 4, 0:C] = vec + early_vec[...]
    bin_sum = bin_sum + early_bin[...]
    grad_in = grad_in + early_in[...]
    grad_out = grad_out + early_out[...]
    for j in range(3):
        lanes = slice(j * LANES, (j + 1) * LANES)
        pack[ROW_BIN + j : ROW_BIN + j + 1, :] = bin_sum[:, lanes]
        pack[ROW_IN + j * C : ROW_IN + (j + 1) * C, :] = grad_in[:, lanes]
        pack[ROW_OUT + j * C : ROW_OUT + (j + 1) * C, :] = grad_out[:, lanes]

    masks, low_back, high_back = row_masks(), row_masks(-low_y), row_masks(-high_y)
    for k, plane in enumerate((0, 1, 6, 7)):
        grads = [gc_ref[plane, x] for x in range(B)]
        move_rows(grads, moved, k, masks)
        move_rows(grads, moved_halo, k, low_back if k < 2 else high_back)

    def kernel_step(b, carry):
        def pairs(a):
            for k, plane in enumerate((0, 1, 6, 7)):
                held = dict(NEAR[plane]).get(a)
                if held is None:
                    grads = [moved[b, k, x] for x in range(B)]
                    yield grads, [source[plane + a - 2, x] for x in range(B)], True
                else:
                    grads = [moved_halo[b, k, x] for x in range(B)]
                    yield grads, [halo[held, 8 + j] for j in range(12)], False

        for a in range(T):
            row = a * T + b
            sums = kernel_taps(pairs(a))
            kernel_rows[row, 0:T, :] = jnp.concatenate(
                [
                    jnp.sum(sums[e] + early_rows[row, e], axis=0, keepdims=True)
                    for e in range(T)
                ],
                axis=0,
            )
        return carry

    lax.fori_loop(0, T, kernel_step, 0)
    for k in range(T * T):
        row = ROW_KERNEL + k * T
        pack[row : row + T, 0:C] = kernel_rows[k, 0:T, :]

    for d in range(parts):
        first = d * chunk
        rows = max(0, min(chunk, ROWS - first))
        if rows:
            packed_ref[d, 0:rows, :] = pack[first : first + rows, :].astype(BF16)
        if rows < chunk:
            packed_ref[d, rows:chunk, :] = jnp.zeros((chunk - rows, LANES), BF16)


def back_kernel(
    odd_ref,
    even_ref,
    source,
    taps,
    gc_ref,
    branch_ref,
    fluid_ref,
    gain_ref,
    bias_ref,
    w_in_ref,
    b_in_ref,
    w_out_ref,
    scale_ref,
    table_vmem,
    up_hbm,
    feat_hbm,
    out_ref,
    mixed_ref,
    table_ref,
    up_ref,
    feat_ref,
    sems,
    rims,
    rim_seeds,
    conv,
    halo,
):
    copies = start_copies(
        sems, (table_vmem, table_ref), (up_hbm, up_ref), (feat_hbm, feat_ref)
    )
    clear_halo(halo, 4)
    from_low, from_high = halo_planes(even_ref, odd_ref)
    for k in range(4):
        below, above = spread(from_low(k)), spread(from_high(k))
        for x in range(B):
            rims[k, x] = below[x]
            rims[4 + k, x] = above[x]
    for k in range(2):
        below, above = spread(from_low(4 + k)), spread(from_high(4 + k))
        for x in range(B):
            rim_seeds[k, x] = below[x]
            rim_seeds[2 + k, x] = above[x]
    copies[0].wait()
    own, low, high, live = layer_places(table_ref)
    low_x, low_y = offset(own, low)
    high_x, high_y = offset(own, high)
    for k in range(2):
        put_halo(halo, k, [source[k, x] for x in range(B)], -low_x)
        put_halo(halo, 2 + k, [source[6 + k, x] for x in range(B)], -high_x)
    masks, low_back, high_back = row_masks(), row_masks(-low_y), row_masks(-high_y)
    for k, (pairs, near, near_masks) in enumerate(
        (
            ([(0, 0), (1, 1), (2, 2), (3, 3)], [(4, 0)], low_back),
            ([(0, 1), (1, 2), (2, 3)], [(3, 0), (4, 1)], low_back),
            ([(2, 4), (3, 5), (4, 6)], [(0, 2), (1, 3)], high_back),
            ([(1, 4), (2, 5), (3, 6), (4, 7)], [(0, 3)], high_back),
        )
    ):
        out = conv_plane(rims, taps, pairs, masks, halo, near, near_masks)
        for x in range(B):
            conv[k, x] = out[x]
    refs = (gain_ref, bias_ref, w_in_ref, b_in_ref, w_out_ref, None, scale_ref)
    grad_conv = dense_part(
        conv[...].reshape(256, C), rim_seeds[...].reshape(256, C), dense_weights(refs), False
    )

    clear_halo(halo, 4)
    for k in range(2):
        put_halo(halo, k, [grad_conv[k, x] for x in range(B)], low_x)
        put_halo(halo, 2 + k, [grad_conv[2 + k, x] for x in range(B)], high_x)
    copies[1].wait()
    copies[2].wait()
    back_taps = Flipped(taps)
    scale_wide = gather_lanes([scale_ref[...]] * B)

    def finish(z, out):
        seed = up_ref[z].astype(F32) * live
        mask = fluid_ref[z].astype(F32) * live
        out_ref[z] = (seed + gather_lanes(out) * mask).astype(BF16)
        wide = gather_lanes([branch_ref[z, x] for x in range(B)])
        mixed_ref[z] = ((feat_ref[z].astype(F32) + scale_wide * wide) * live).astype(BF16)

    def middle_step(z, carry):
        finish(2 + z, middle_plane(gc_ref, back_taps, z, masks))
        return carry

    lax.fori_loop(0, 4, middle_step, 0)
    low_masks, high_masks = row_masks(low_y), row_masks(high_y)
    for z in (0, 1, 6, 7):
        near = low_masks if z < 2 else high_masks
        finish(z, conv_plane(gc_ref, back_taps, own_pairs(z), masks, halo, NEAR[z], near))


def reduce_kernel(parts, factor, got_ref, out_ref):
    def add(d, total):
        return total + got_ref[d].astype(F32)

    total = lax.fori_loop(0, parts, add, jnp.zeros(got_ref.shape[1:], F32), unroll=8)
    total = (total * factor).astype(BF16)

    def copy(d, carry):
        out_ref[d] = total
        return carry

    lax.fori_loop(0, parts, copy, 0, unroll=8)


def unpack_kernel(chunk, got_ref, kernel_ref, in_ref, out_ref, bin_ref, vec_ref, pack):
    for d in range(got_ref.shape[0]):
        first = d * chunk
        if first >= ROWS:
            break
        rows = min(chunk, ROWS - first)
        pack[first : first + rows, :] = got_ref[d, 0:rows, :].astype(F32)
    for j in range(3):
        lanes = slice(j * LANES, (j + 1) * LANES)
        in_ref[:, lanes] = pack[ROW_IN + j * C : ROW_IN + (j + 1) * C, :]
        out_ref[:, lanes] = pack[ROW_OUT + j * C : ROW_OUT + (j + 1) * C, :]
        bin_ref[lanes] = pack[ROW_BIN + j, :]
    vec_ref[...] = pack[ROW_VEC : ROW_VEC + 4, 0:C]
    for a in range(T):
        for b in range(T):
            row = ROW_KERNEL + (a * T + b) * T
            kernel_ref[a, b] = pack[row : row + T, 0:C]


def local(
    features,
    wall_mask,
    block_positions,
    dw_kernel,
    norm_gain,
    norm_bias,
    w_in,
    b_in,
    w_out,
    b_out,
    layer_scale,
    upstream,
):
    feat = features[0, 0, 0]
    walls = wall_mask[0, 0, 0]
    up = upstream[0, 0, 0]
    table = block_positions[0, :, 0]
    layers = lax.axis_size("space")
    parts = layers * lax.axis_size("sample")
    chunk = 8 * (-(-ROWS // (8 * parts)))
    block = (B, B, B * C)

    held = [pinned(array) for array in (table, feat, walls, up, dw_kernel)]
    for_even, for_odd, masked, fluid, dw = pl.pallas_call(
        send_kernel,
        out_shape=[
            jax.ShapeDtypeStruct((6, B, B * C), BF16),
            jax.ShapeDtypeStruct((6, B, B * C), BF16),
            jax.ShapeDtypeStruct(block, BF16),
            jax.ShapeDtypeStruct(block, BF16),
            jax.ShapeDtypeStruct((T, T, T, C), F32),
        ],
        in_specs=[hbm()] * 5,
        out_specs=[vmem()] * 5,
        scratch_shapes=[
            pltpu.SMEM((layers,), jnp.int32),
            pltpu.VMEM(block, BF16),
            pltpu.VMEM((B, B * B), jnp.int32),
            pltpu.VMEM(block, BF16),
            pltpu.SemaphoreType.DMA((5,)),
        ],
        compiler_params=params(),
        name="send",
    )(*held)

    def swap(array, first):
        pairs = [(i, i + 1) for i in range(first, layers - 1, 2)]
        return lax.ppermute(array, "space", pairs + [(j, i) for i, j in pairs])

    odd = swap(for_odd, 1)
    even = swap(for_even, 0)

    weights = [
        norm_gain.reshape(1, C),
        norm_bias.reshape(1, C),
        w_in,
        b_in,
        w_out.T,
        b_out.reshape(1, C),
        layer_scale.reshape(1, C),
    ]
    operands = [pinned(array) for array in [table, up] + weights]
    source, seeds, taps, conv, *held = pl.pallas_call(
        early_kernel,
        out_shape=[
            jax.ShapeDtypeStruct((B, B, B, C), F32),
            jax.ShapeDtypeStruct((B, B, B, C), F32),
            jax.ShapeDtypeStruct((T, T, T, B, C), F32),
            jax.ShapeDtypeStruct((B, B, B, C), F32),
        ]
        + [jax.ShapeDtypeStruct(array.shape, array.dtype) for array in weights]
        + [
            jax.ShapeDtypeStruct((4, B, B, C), F32),
            jax.ShapeDtypeStruct((4, B, B, C), F32),
            jax.ShapeDtypeStruct((C, HID), F32),
            jax.ShapeDtypeStruct((C, HID), F32),
            jax.ShapeDtypeStruct((4, C), F32),
            jax.ShapeDtypeStruct((1, HID), F32),
            jax.ShapeDtypeStruct((T * T, T, B, C), F32),
            jax.ShapeDtypeStruct((layers,), jnp.int32),
        ],
        in_specs=[vmem()] * 2 + [hbm()] * len(operands),
        out_specs=[vmem()] * (12 + len(weights)),
        scratch_shapes=[
            pltpu.SMEM((layers,), jnp.int32),
            pltpu.VMEM(block, BF16),
            pltpu.VMEM((T, 4, B, B, C), F32),
            pltpu.SemaphoreType.DMA((len(operands) + 1,)),
        ],
        compiler_params=params(),
        cost_estimate=pl.CostEstimate(flops=40_000_000, bytes_accessed=800_000, transcendentals=0),
        name="early",
    )(masked, dw, *operands)

    branch, grad_conv, packed = pl.pallas_call(
        functools.partial(main_kernel, chunk, parts),
        out_shape=[
            jax.ShapeDtypeStruct((B, B, B, C), F32),
            jax.ShapeDtypeStruct((B, B, B, C), F32),
            jax.ShapeDtypeStruct((parts, chunk, LANES), BF16),
        ],
        in_specs=[vmem()] * (6 + len(held)),
        out_specs=[vmem()] * 3,
        scratch_shapes=[
            pltpu.SMEM((layers,), jnp.int32),
            pltpu.SemaphoreType.DMA((1,)),
            pltpu.VMEM((4, 28, B, C), F32),
            pltpu.VMEM((4, B, B, C), F32),
            pltpu.VMEM((T, 4, B, B, C), F32),
            pltpu.VMEM((T, 4, B, B, C), F32),
            pltpu.VMEM((T * T, B, C), F32),
            pltpu.VMEM((ROWS, LANES), F32),
        ],
        compiler_params=params(),
        name="main",
    )(odd, even, source, seeds, taps, conv, *held)

    axes = ("space", "sample")
    scattered = lax.all_to_all(packed, axes, 0, 0, tiled=True)

    weights = held[:5] + held[6:7]
    grad_field, mixed = pl.pallas_call(
        back_kernel,
        out_shape=[jax.ShapeDtypeStruct(block, BF16)] * 2,
        in_specs=[vmem()] * (8 + len(weights)) + [hbm()] * 2,
        out_specs=[vmem()] * 2,
        scratch_shapes=[
            pltpu.SMEM((layers,), jnp.int32),
            pltpu.VMEM(block, BF16),
            pltpu.VMEM(block, BF16),
            pltpu.SemaphoreType.DMA((3,)),
            pltpu.VMEM((8, B, B, C), F32),
            pltpu.VMEM((4, B, B, C), F32),
            pltpu.VMEM((4, B, B, C), F32),
            pltpu.VMEM((4, 28, B, C), F32),
        ],
        compiler_params=params(),
        cost_estimate=pl.CostEstimate(flops=60_000_000, bytes_accessed=800_000, transcendentals=0),
        name="back",
    )(
        odd,
        even,
        source,
        taps,
        grad_conv,
        branch,
        fluid,
        *weights,
        held[-1],
        *[pinned(array) for array in (up, feat)],
    )

    factor = 1.0 / math.sqrt(parts * B**3)
    summed = pl.pallas_call(
        functools.partial(reduce_kernel, parts, factor),
        out_shape=jax.ShapeDtypeStruct((parts, chunk, LANES), BF16),
        in_specs=[vmem()],
        out_specs=vmem(),
        compiler_params=params(),
        name="reduce",
    )(scattered)
    gathered = lax.all_to_all(summed, axes, 0, 0, tiled=True)
    grad_kernel, grad_w_in, grad_w_out, grad_b_in, grad_vectors = pl.pallas_call(
        functools.partial(unpack_kernel, chunk),
        out_shape=[
            jax.ShapeDtypeStruct((T, T, T, C), F32),
            jax.ShapeDtypeStruct((C, HID), F32),
            jax.ShapeDtypeStruct((C, HID), F32),
            jax.ShapeDtypeStruct((HID,), F32),
            jax.ShapeDtypeStruct((4, C), F32),
        ],
        in_specs=[vmem()],
        out_specs=[vmem()] * 5,
        scratch_shapes=[pltpu.VMEM((ROWS, LANES), F32)],
        compiler_params=params(),
        name="unpack",
    )(gathered)
    lead = (1, 1, 1)
    return (
        mixed.reshape(lead + block),
        grad_field.reshape(lead + block),
        grad_kernel,
        grad_w_in,
        grad_w_out.T,
        grad_b_in,
        grad_vectors,
    )


def solution(mesh):
    return jax.shard_map(
        local,
        mesh=mesh,
        in_specs=(
            P("sample", "space", None, None, None, None),
            P("sample", "space", None, None, None),
            P("sample", None, None),
            P(),
            P(),
            P(),
            P(),
            P(),
            P(),
            P(),
            P(),
            P("sample", "space", None, None, None, None),
        ),
        out_specs=(
            P("sample", "space", None, None, None, None),
            P("sample", "space", None, None, None, None),
            P(),
            P(),
            P(),
            P(),
            P(),
        ),
        check_vma=False,
    )
```

```python
import functools
import math

import jax
import jax.numpy as jnp
from jax import lax
from jax.experimental import pallas as pl
from jax.experimental.pallas import tpu as pltpu
from jax.sharding import PartitionSpec as P

GELU_SCALE = 0.7978845608028654
GELU_CUBIC = 0.044715
NORM_EPS = 1e-06

B = 8
T = 5
C = 96
HID = 384
LANES = 128

ROW_IN = 0
ROW_OUT = 288
ROW_KERNEL = 576
ROW_BIN = 704
ROW_VEC = 707
ROWS = 712

F32 = jnp.float32
BF16 = jnp.bfloat16

VMEM_LIMIT = 48 * 1024 * 1024


def params():
    return pltpu.CompilerParams(vmem_limit_bytes=VMEM_LIMIT)


def vmem():
    return pl.BlockSpec(memory_space=pltpu.VMEM)


def hbm():
    return pl.BlockSpec(memory_space=pltpu.HBM)


def pinned(array):
    return pltpu.with_memory_space_constraint(array, pltpu.HBM)


def start_copies(sems, *pairs):
    copies = [
        pltpu.make_async_copy(source, target, sems.at[k])
        for k, (source, target) in enumerate(pairs)
    ]
    for copy in copies:
        copy.start()
    return copies


def layer_places(table_ref):
    layer = lax.axis_index("space")
    count = lax.axis_size("space")
    own = table_ref[layer]
    low = table_ref[jnp.maximum(layer - 1, 0)]
    high = table_ref[jnp.minimum(layer + 1, count - 1)]
    live = jnp.where(own >= 0, 1.0, 0.0).astype(F32)
    return jnp.maximum(own, 0), jnp.maximum(low, 0), jnp.maximum(high, 0), live


def is_even():
    return (lax.axis_index("space") & 1) == 0


def halo_planes(even_ref, odd_ref):
    even = is_even()

    def low(k):
        return jnp.where(even, odd_ref[k].astype(F32), even_ref[k].astype(F32))

    def high(k):
        return jnp.where(even, even_ref[k].astype(F32), odd_ref[k].astype(F32))

    return low, high


def offset(own, other):
    dy = (other >> 1) - (own >> 1)
    dx = (other & 1) - (own & 1)
    return 8 * dx, 8 * dy


def spread(field):
    return [field[:, x * C : (x + 1) * C] for x in range(B)]


def gather_lanes(parts):
    return jnp.concatenate(parts, axis=-1)


def send_kernel(
    table_hbm,
    feat_hbm,
    wall_hbm,
    up_hbm,
    dw_hbm,
    even_ref,
    odd_ref,
    masked_ref,
    fluid_ref,
    dw_ref,
    table_ref,
    feat_ref,
    wall_ref,
    up_ref,
    sems,
):
    copies = start_copies(
        sems,
        (wall_hbm, wall_ref),
        (feat_hbm, feat_ref),
        (up_hbm, up_ref),
        (table_hbm, table_ref),
        (dw_hbm, dw_ref),
    )
    copies[3].wait()
    _, _, _, live = layer_places(table_ref)
    copies[0].wait()
    walls = wall_ref[...]
    fluid = (1 - walls).astype(F32)
    row = lax.broadcasted_iota(jnp.int32, (B, B * B), 0)
    lane = lax.broadcasted_iota(jnp.int32, (B, B * B), 1)
    pick = (lane >> 3) == row
    tall = jnp.concatenate(
        [jnp.where(pick, fluid[z : z + 1, :], 0.0) for z in range(B)], axis=0
    ).astype(BF16)
    src = lax.broadcasted_iota(jnp.int32, (B * B, B * C), 0) & 7
    dst = lax.broadcasted_iota(jnp.int32, (B * B, B * C), 1)
    widen = jnp.where((dst >= src * C) & (dst < src * C + C), 1.0, 0.0).astype(BF16)
    wide = jnp.dot(tall, widen, preferred_element_type=F32)
    copies[1].wait()
    copies[2].wait()
    for z in range(B):
        fluid_z = wide[z * B : (z + 1) * B, :]
        fluid_ref[z] = fluid_z.astype(BF16)
        masked = (feat_ref[z].astype(F32) * (fluid_z * live)).astype(BF16)
        masked_ref[z] = masked

    def payload(target, first):
        target[0:4] = masked_ref[first : first + 4]
        for k in range(2):
            plane = k if first == 0 else 6 + k
            target[4 + k] = (up_ref[plane].astype(F32) * live).astype(BF16)

    @pl.when(is_even())
    def _():
        payload(even_ref, 4)
        payload(odd_ref, 0)

    @pl.when(jnp.logical_not(is_even()))
    def _():
        payload(even_ref, 0)
        payload(odd_ref, 4)

    copies[4].wait()


def wide_taps(dw_ref, taps):
    for a in range(T):
        for b in range(T):
            for e in range(T):
                taps[a, b, e] = jnp.broadcast_to(dw_ref[a, b, e : e + 1, :], (B, C))


class Flipped:
    def __init__(self, taps):
        self.taps = taps

    def __getitem__(self, index):
        a, b, e = index
        return self.taps[T - 1 - a, T - 1 - b, T - 1 - e]


def rows_of():
    return lax.broadcasted_iota(jnp.int32, (B, C), 0)


def put_halo(halo, plane, parts, start):
    for x in range(B):
        halo[plane, start + 10 + x] = parts[x]


def clear_halo(halo, planes):
    for p in range(planes):
        halo[p, 8:20] = jnp.zeros((12, B, C), F32)


def add_own(acc, window, taps, a, b):
    for e in range(T):
        weight = taps[a, b, e]
        for x in range(B):
            if 0 <= x + e - 2 < B:
                acc[x] = acc[x] + window[x + e - 2] * weight


def add_halo(acc, window, taps, a, b):
    for e in range(T):
        weight = taps[a, b, e]
        for x in range(B):
            acc[x] = acc[x] + window[x + e] * weight


def shift_rows(value, by, start):
    row = rows_of() + (by - start)
    rolled = value if by == 0 else pltpu.roll(value, (-by) % B, 0)
    return jnp.where((row >= 0) & (row < B), rolled, 0.0)


def conv_plane(source, taps, own, halo=None, halos=(), start=0):
    out = [jnp.zeros((B, C), F32) for _ in range(B)]
    for b in range(T):
        if own:
            acc = [jnp.zeros((B, C), F32) for _ in range(B)]
            for a, plane in own:
                add_own(acc, [source[plane, x] for x in range(B)], taps, a, b)
            for x in range(B):
                out[x] = out[x] + shift_rows(acc[x], b - 2, 0)
        if halos:
            acc = [jnp.zeros((B, C), F32) for _ in range(B)]
            for a, plane in halos:
                add_halo(acc, [halo[plane, 8 + j] for j in range(12)], taps, a, b)
            for x in range(B):
                out[x] = out[x] + shift_rows(acc[x], b - 2, start)
    return out


def middle_plane(source, taps, first):
    return conv_plane(source, taps, [(a, first + a) for a in range(T)])


OWN_TAPS = {0: (2, 3, 4), 1: (1, 2, 3, 4), 6: (0, 1, 2, 3), 7: (0, 1, 2)}


def own_pairs(plane):
    return [(a, plane + a - 2) for a in OWN_TAPS.get(plane, range(T))]


def dense_weights(refs):
    gain, bias, w_in, b_in, w_out, b_out, scale = refs
    b_out = None if b_out is None else b_out[...]
    return (
        gain[...],
        bias[...],
        w_in[...],
        b_in[...].reshape(1, HID),
        w_out[...],
        b_out,
        scale[...],
    )


def dense_part(conv_rows, seed, weights, own=True):
    gain, bias, w_in, b_in, w_out_t, b_out, scale = weights
    mean = jnp.sum(conv_rows, axis=1, keepdims=True) * (1.0 / C)
    centred = conv_rows - mean
    var = jnp.sum(centred * centred, axis=1, keepdims=True) * (1.0 / C)
    inv_std = lax.rsqrt(var + NORM_EPS)
    unit = centred * inv_std
    normed = (unit * gain + bias).astype(BF16)
    pre = jnp.dot(normed, w_in, preferred_element_type=F32) + b_in
    square = pre * pre
    inner = pre * (GELU_SCALE + (GELU_SCALE * GELU_CUBIC) * square)
    tanh = jnp.tanh(inner)
    half = 0.5 + 0.5 * tanh
    slope = half + (0.5 * pre) * (1.0 - tanh * tanh) * (
        GELU_SCALE + (3.0 * GELU_SCALE * GELU_CUBIC) * square
    )
    grad_branch = (seed * scale).astype(BF16)
    grad_act = jnp.dot(grad_branch, w_out_t, preferred_element_type=F32)
    grad_pre = (grad_act * slope).astype(BF16)
    grad_normed = lax.dot_general(
        grad_pre, w_in, (((1,), (1,)), ((), ())), preferred_element_type=F32
    )
    scaled = grad_normed * gain
    mean_s = jnp.sum(scaled, axis=1, keepdims=True) * (1.0 / C)
    mean_su = jnp.sum(scaled * unit, axis=1, keepdims=True) * (1.0 / C)
    grad_conv = inv_std * (scaled - mean_s - unit * mean_su)
    grad_conv = grad_conv.astype(BF16).astype(F32).reshape(-1, B, B, C)
    if not own:
        return grad_conv
    activated = (pre * half).astype(BF16)
    branch = (
        lax.dot_general(activated, w_out_t, (((1,), (1,)), ((), ())), preferred_element_type=F32)
        + b_out
    )
    grad_in = lax.dot_general(
        normed, grad_pre, (((0,), (0,)), ((), ())), preferred_element_type=F32
    )
    grad_out = lax.dot_general(
        grad_branch, activated, (((0,), (0,)), ((), ())), preferred_element_type=F32
    )
    vec = jnp.concatenate(
        [
            jnp.sum(grad_normed * unit, axis=0, keepdims=True),
            jnp.sum(grad_normed, axis=0, keepdims=True),
            jnp.sum(grad_branch.astype(F32), axis=0, keepdims=True),
            jnp.sum(seed * branch, axis=0, keepdims=True),
        ],
        axis=0,
    )
    bin_sum = jnp.sum(grad_pre.astype(F32), axis=0, keepdims=True)
    return grad_conv, branch.reshape(-1, B, B, C), grad_in, grad_out, vec, bin_sum


def kernel_taps(pairs):
    acc = [[jnp.zeros((B, C), F32) for _ in range(2)] for _ in range(T)]
    for grads, window, inside in pairs:
        for e in range(T):
            for x in range(B):
                if inside:
                    if not 0 <= x + e - 2 < B:
                        continue
                    value = window[x + e - 2]
                else:
                    value = window[x + e]
                acc[e][x & 1] = acc[e][x & 1] + value * grads[x]
    return jnp.concatenate(
        [jnp.sum(pair[0] + pair[1], axis=0, keepdims=True) for pair in acc], axis=0
    )


def move_rows(grads, moved, k):
    for x in range(B):
        for b in range(T):
            moved[b, k, x] = shift_rows(grads[x], 2 - b, 0)


def early_kernel(
    masked_ref,
    dw_ref,
    table_hbm,
    up_hbm,
    gain_hbm,
    bias_hbm,
    w_in_hbm,
    b_in_hbm,
    w_out_hbm,
    b_out_hbm,
    scale_hbm,
    source,
    seeds,
    taps,
    conv,
    gain_ref,
    bias_ref,
    w_in_ref,
    b_in_ref,
    w_out_ref,
    b_out_ref,
    scale_ref,
    gc_ref,
    branch_ref,
    grad_in_ref,
    grad_out_ref,
    vec_ref,
    bin_ref,
    rows_ref,
    table_vmem,
    table_ref,
    up_ref,
    moved,
    sems,
):
    copies = start_copies(
        sems,
        (table_hbm, table_ref),
        (up_hbm, up_ref),
        (gain_hbm, gain_ref),
        (bias_hbm, bias_ref),
        (w_in_hbm, w_in_ref),
        (b_in_hbm, b_in_ref),
        (w_out_hbm, w_out_ref),
        (b_out_hbm, b_out_ref),
        (scale_hbm, scale_ref),
        (table_hbm, table_vmem),
    )

    def own_planes(z, carry):
        field = spread(masked_ref[z].astype(F32))
        for x in range(B):
            source[z, x] = field[x]
        return carry

    lax.fori_loop(0, B, own_planes, 0, unroll=True)
    wide_taps(dw_ref, taps)

    def middle_step(z, carry):
        out = middle_plane(source, taps, z)
        for x in range(B):
            conv[2 + z, x] = out[x]
        return carry

    lax.fori_loop(0, 4, middle_step, 0)

    def edge(plane):
        out = conv_plane(source, taps, own_pairs(plane))
        for x in range(B):
            conv[plane, x] = out[x]

    for plane in (0, 1, 6, 7):
        edge(plane)
    for copy in copies:
        copy.wait()
    live = layer_places(table_ref)[3]

    def own_seeds(z, carry):
        seed = spread(up_ref[z].astype(F32) * live)
        for x in range(B):
            seeds[z, x] = seed[x]
        return carry

    lax.fori_loop(0, B, own_seeds, 0, unroll=True)
    refs = (gain_ref, bias_ref, w_in_ref, b_in_ref, w_out_ref, b_out_ref, scale_ref)
    grad_conv, branch, grad_in, grad_out, vec, bin_sum = dense_part(
        conv[2:6].reshape(256, C), seeds[2:6].reshape(256, C), dense_weights(refs)
    )
    gc_ref[...] = grad_conv
    branch_ref[...] = branch
    grad_in_ref[...] = grad_in
    grad_out_ref[...] = grad_out
    vec_ref[...] = vec
    bin_ref[...] = bin_sum

    for k in range(4):
        move_rows([gc_ref[k, x] for x in range(B)], moved, k)

    def kernel_step(b, carry):
        for a in range(T):
            rows_ref[a * T + b, 0:T, :] = kernel_taps(
                (
                    [moved[b, k, x] for x in range(B)],
                    [source[k + a, x] for x in range(B)],
                    True,
                )
                for k in range(4)
            )
        return carry

    lax.fori_loop(0, T, kernel_step, 0)


NEAR = {0: [(0, 0), (1, 1)], 1: [(0, 1)], 6: [(4, 2)], 7: [(3, 2), (4, 3)]}


def main_kernel(
    chunk,
    parts,
    odd_ref,
    even_ref,
    source,
    seeds,
    taps,
    conv_ref,
    gain_ref,
    bias_ref,
    w_in_ref,
    b_in_ref,
    w_out_ref,
    b_out_ref,
    scale_ref,
    early_gc,
    early_branch,
    early_in,
    early_out,
    early_vec,
    early_bin,
    early_rows,
    table_vmem,
    branch_ref,
    gc_ref,
    packed_ref,
    table_ref,
    sems,
    halo,
    conv,
    moved,
    moved_halo,
    kernel_rows,
    pack,
):
    copies = start_copies(sems, (table_vmem, table_ref))
    clear_halo(halo, 4)
    pack[ROW_KERNEL:ROWS, :] = jnp.zeros((ROWS - ROW_KERNEL, LANES), F32)
    gc_ref[2:6] = early_gc[...]
    branch_ref[2:6] = early_branch[...]

    from_low, from_high = halo_planes(even_ref, odd_ref)
    below = [spread(from_low(2 + k)) for k in range(2)]
    above = [spread(from_high(k)) for k in range(2)]
    copies[0].wait()
    own, low, high, _ = layer_places(table_ref)
    low_x, low_y = offset(own, low)
    high_x, high_y = offset(own, high)
    for k in range(2):
        put_halo(halo, k, below[k], low_x)
        put_halo(halo, 2 + k, above[k], high_x)
    for k, plane in enumerate((0, 1, 6, 7)):
        out = conv_plane(source, taps, [], halo, NEAR[plane], low_y if k < 2 else high_y)
        for x in range(B):
            conv[k, x] = conv_ref[plane, x] + out[x]

    late = jnp.concatenate([seeds[0:2], seeds[6:8]], axis=0)
    refs = (gain_ref, bias_ref, w_in_ref, b_in_ref, w_out_ref, b_out_ref, scale_ref)
    grad_conv, branch, grad_in, grad_out, vec, bin_sum = dense_part(
        conv[...].reshape(256, C), late.reshape(256, C), dense_weights(refs)
    )
    gc_ref[0:2] = grad_conv[0:2]
    gc_ref[6:8] = grad_conv[2:4]
    branch_ref[0:2] = branch[0:2]
    branch_ref[6:8] = branch[2:4]
    pack[ROW_VEC : ROW_VEC + 4, 0:C] = vec + early_vec[...]
    bin_sum = bin_sum + early_bin[...]
    grad_in = grad_in + early_in[...]
    grad_out = grad_out + early_out[...]
    for j in range(3):
        lanes = slice(j * LANES, (j + 1) * LANES)
        pack[ROW_BIN + j : ROW_BIN + j + 1, :] = bin_sum[:, lanes]
        pack[ROW_IN + j * C : ROW_IN + (j + 1) * C, :] = grad_in[:, lanes]
        pack[ROW_OUT + j * C : ROW_OUT + (j + 1) * C, :] = grad_out[:, lanes]

    for k, plane in enumerate((0, 1, 6, 7)):
        grads = [gc_ref[plane, x] for x in range(B)]
        move_rows(grads, moved, k)
        start = low_y if k < 2 else high_y
        for x in range(B):
            for b in range(T):
                moved_halo[b, k, x] = shift_rows(grads[x], 2 - b, -start)

    def kernel_step(b, carry):
        def pairs(a):
            for k, plane in enumerate((0, 1, 6, 7)):
                held = dict(NEAR[plane]).get(a)
                if held is None:
                    grads = [moved[b, k, x] for x in range(B)]
                    yield grads, [source[plane + a - 2, x] for x in range(B)], True
                else:
                    grads = [moved_halo[b, k, x] for x in range(B)]
                    yield grads, [halo[held, 8 + j] for j in range(12)], False

        for a in range(T):
            row = a * T + b
            kernel_rows[row, 0:T, :] = early_rows[row, 0:T, :] + kernel_taps(pairs(a))
        return carry

    lax.fori_loop(0, T, kernel_step, 0)
    for k in range(T * T):
        row = ROW_KERNEL + k * T
        pack[row : row + T, 0:C] = kernel_rows[k, 0:T, :]

    for d in range(parts):
        first = d * chunk
        rows = max(0, min(chunk, ROWS - first))
        if rows:
            packed_ref[d, 0:rows, :] = pack[first : first + rows, :].astype(BF16)
        if rows < chunk:
            packed_ref[d, rows:chunk, :] = jnp.zeros((chunk - rows, LANES), BF16)


def back_kernel(
    odd_ref,
    even_ref,
    source,
    taps,
    gc_ref,
    branch_ref,
    fluid_ref,
    gain_ref,
    bias_ref,
    w_in_ref,
    b_in_ref,
    w_out_ref,
    scale_ref,
    table_vmem,
    up_hbm,
    feat_hbm,
    out_ref,
    mixed_ref,
    table_ref,
    up_ref,
    feat_ref,
    sems,
    rims,
    rim_seeds,
    conv,
    halo,
):
    copies = start_copies(
        sems, (table_vmem, table_ref), (up_hbm, up_ref), (feat_hbm, feat_ref)
    )
    clear_halo(halo, 4)
    from_low, from_high = halo_planes(even_ref, odd_ref)
    for k in range(4):
        below, above = spread(from_low(k)), spread(from_high(k))
        for x in range(B):
            rims[k, x] = below[x]
            rims[4 + k, x] = above[x]
    for k in range(2):
        below, above = spread(from_low(4 + k)), spread(from_high(4 + k))
        for x in range(B):
            rim_seeds[k, x] = below[x]
            rim_seeds[2 + k, x] = above[x]
    copies[0].wait()
    own, low, high, live = layer_places(table_ref)
    low_x, low_y = offset(own, low)
    high_x, high_y = offset(own, high)
    for k in range(2):
        put_halo(halo, k, [source[k, x] for x in range(B)], -low_x)
        put_halo(halo, 2 + k, [source[6 + k, x] for x in range(B)], -high_x)
    for k, (pairs, near, start) in enumerate(
        (
            ([(0, 0), (1, 1), (2, 2), (3, 3)], [(4, 0)], -low_y),
            ([(0, 1), (1, 2), (2, 3)], [(3, 0), (4, 1)], -low_y),
            ([(2, 4), (3, 5), (4, 6)], [(0, 2), (1, 3)], -high_y),
            ([(1, 4), (2, 5), (3, 6), (4, 7)], [(0, 3)], -high_y),
        )
    ):
        out = conv_plane(rims, taps, pairs, halo, near, start)
        for x in range(B):
            conv[k, x] = out[x]
    refs = (gain_ref, bias_ref, w_in_ref, b_in_ref, w_out_ref, None, scale_ref)
    grad_conv = dense_part(
        conv[...].reshape(256, C), rim_seeds[...].reshape(256, C), dense_weights(refs), False
    )

    clear_halo(halo, 4)
    for k in range(2):
        put_halo(halo, k, [grad_conv[k, x] for x in range(B)], low_x)
        put_halo(halo, 2 + k, [grad_conv[2 + k, x] for x in range(B)], high_x)
    copies[1].wait()
    copies[2].wait()
    back_taps = Flipped(taps)
    scale_wide = gather_lanes([scale_ref[...]] * B)

    def finish(z, out):
        seed = up_ref[z].astype(F32) * live
        mask = fluid_ref[z].astype(F32) * live
        out_ref[z] = (seed + gather_lanes(out) * mask).astype(BF16)
        wide = gather_lanes([branch_ref[z, x] for x in range(B)])
        mixed_ref[z] = ((feat_ref[z].astype(F32) + scale_wide * wide) * live).astype(BF16)

    def middle_step(z, carry):
        finish(2 + z, middle_plane(gc_ref, back_taps, z))
        return carry

    lax.fori_loop(0, 4, middle_step, 0)
    for z in (0, 1, 6, 7):
        start = low_y if z < 2 else high_y
        finish(z, conv_plane(gc_ref, back_taps, own_pairs(z), halo, NEAR[z], start))


def reduce_kernel(parts, factor, got_ref, after_ref, out_ref):
    def add(d, total):
        return total + got_ref[d].astype(F32)

    total = lax.fori_loop(0, parts, add, jnp.zeros(got_ref.shape[1:], F32), unroll=8)
    total = (total * factor).astype(BF16)

    def copy(d, carry):
        out_ref[d] = total
        return carry

    lax.fori_loop(0, parts, copy, 0, unroll=8)


def unpack_kernel(chunk, got_ref, kernel_ref, in_ref, out_ref, bin_ref, vec_ref, pack):
    for d in range(got_ref.shape[0]):
        first = d * chunk
        if first >= ROWS:
            break
        rows = min(chunk, ROWS - first)
        pack[first : first + rows, :] = got_ref[d, 0:rows, :].astype(F32)
    for j in range(3):
        lanes = slice(j * LANES, (j + 1) * LANES)
        in_ref[:, lanes] = pack[ROW_IN + j * C : ROW_IN + (j + 1) * C, :]
        out_ref[:, lanes] = pack[ROW_OUT + j * C : ROW_OUT + (j + 1) * C, :]
        bin_ref[lanes] = pack[ROW_BIN + j, :]
    vec_ref[...] = pack[ROW_VEC : ROW_VEC + 4, 0:C]
    for a in range(T):
        for b in range(T):
            row = ROW_KERNEL + (a * T + b) * T
            kernel_ref[a, b] = pack[row : row + T, 0:C]


def local(
    features,
    wall_mask,
    block_positions,
    dw_kernel,
    norm_gain,
    norm_bias,
    w_in,
    b_in,
    w_out,
    b_out,
    layer_scale,
    upstream,
):
    feat = features[0, 0, 0]
    walls = wall_mask[0, 0, 0]
    up = upstream[0, 0, 0]
    table = block_positions[0, :, 0]
    layers = lax.axis_size("space")
    parts = layers * lax.axis_size("sample")
    chunk = 8 * (-(-ROWS // (8 * parts)))
    block = (B, B, B * C)

    held = [pinned(array) for array in (table, feat, walls, up, dw_kernel)]
    for_even, for_odd, masked, fluid, dw = pl.pallas_call(
        send_kernel,
        out_shape=[
            jax.ShapeDtypeStruct((6, B, B * C), BF16),
            jax.ShapeDtypeStruct((6, B, B * C), BF16),
            jax.ShapeDtypeStruct(block, BF16),
            jax.ShapeDtypeStruct(block, BF16),
            jax.ShapeDtypeStruct((T, T, T, C), F32),
        ],
        in_specs=[hbm()] * 5,
        out_specs=[vmem()] * 5,
        scratch_shapes=[
            pltpu.SMEM((layers,), jnp.int32),
            pltpu.VMEM(block, BF16),
            pltpu.VMEM((B, B * B), jnp.int32),
            pltpu.VMEM(block, BF16),
            pltpu.SemaphoreType.DMA((5,)),
        ],
        compiler_params=params(),
        name="send",
    )(*held)

    def swap(array, first):
        pairs = [(i, i + 1) for i in range(first, layers - 1, 2)]
        return lax.ppermute(array, "space", pairs + [(j, i) for i, j in pairs])

    odd = swap(for_odd, 1)
    even = swap(for_even, 0)

    weights = [
        norm_gain.reshape(1, C),
        norm_bias.reshape(1, C),
        w_in,
        b_in,
        w_out.T,
        b_out.reshape(1, C),
        layer_scale.reshape(1, C),
    ]
    operands = [pinned(array) for array in [table, up] + weights]
    source, seeds, taps, conv, *held = pl.pallas_call(
        early_kernel,
        out_shape=[
            jax.ShapeDtypeStruct((B, B, B, C), F32),
            jax.ShapeDtypeStruct((B, B, B, C), F32),
            jax.ShapeDtypeStruct((T, T, T, B, C), F32),
            jax.ShapeDtypeStruct((B, B, B, C), F32),
        ]
        + [jax.ShapeDtypeStruct(array.shape, array.dtype) for array in weights]
        + [
            jax.ShapeDtypeStruct((4, B, B, C), F32),
            jax.ShapeDtypeStruct((4, B, B, C), F32),
            jax.ShapeDtypeStruct((C, HID), F32),
            jax.ShapeDtypeStruct((C, HID), F32),
            jax.ShapeDtypeStruct((4, C), F32),
            jax.ShapeDtypeStruct((1, HID), F32),
            jax.ShapeDtypeStruct((T * T, B, C), F32),
            jax.ShapeDtypeStruct((layers,), jnp.int32),
        ],
        in_specs=[vmem()] * 2 + [hbm()] * len(operands),
        out_specs=[vmem()] * (12 + len(weights)),
        scratch_shapes=[
            pltpu.SMEM((layers,), jnp.int32),
            pltpu.VMEM(block, BF16),
            pltpu.VMEM((T, 4, B, B, C), F32),
            pltpu.SemaphoreType.DMA((len(operands) + 1,)),
        ],
        compiler_params=params(),
        cost_estimate=pl.CostEstimate(flops=40_000_000, bytes_accessed=800_000, transcendentals=0),
        name="early",
    )(masked, dw, *operands)

    branch, grad_conv, packed = pl.pallas_call(
        functools.partial(main_kernel, chunk, parts),
        out_shape=[
            jax.ShapeDtypeStruct((B, B, B, C), F32),
            jax.ShapeDtypeStruct((B, B, B, C), F32),
            jax.ShapeDtypeStruct((parts, chunk, LANES), BF16),
        ],
        in_specs=[vmem()] * (6 + len(held)),
        out_specs=[vmem()] * 3,
        scratch_shapes=[
            pltpu.SMEM((layers,), jnp.int32),
            pltpu.SemaphoreType.DMA((1,)),
            pltpu.VMEM((4, 28, B, C), F32),
            pltpu.VMEM((4, B, B, C), F32),
            pltpu.VMEM((T, 4, B, B, C), F32),
            pltpu.VMEM((T, 4, B, B, C), F32),
            pltpu.VMEM((T * T, B, C), F32),
            pltpu.VMEM((ROWS, LANES), F32),
        ],
        compiler_params=params(),
        name="main",
    )(odd, even, source, seeds, taps, conv, *held)

    axes = ("space", "sample")
    scattered = lax.all_to_all(packed, axes, 0, 0, tiled=True)

    weights = held[:5] + held[6:7]
    grad_field, mixed = pl.pallas_call(
        back_kernel,
        out_shape=[jax.ShapeDtypeStruct(block, BF16)] * 2,
        in_specs=[vmem()] * (8 + len(weights)) + [hbm()] * 2,
        out_specs=[vmem()] * 2,
        scratch_shapes=[
            pltpu.SMEM((layers,), jnp.int32),
            pltpu.VMEM(block, BF16),
            pltpu.VMEM(block, BF16),
            pltpu.SemaphoreType.DMA((3,)),
            pltpu.VMEM((8, B, B, C), F32),
            pltpu.VMEM((4, B, B, C), F32),
            pltpu.VMEM((4, B, B, C), F32),
            pltpu.VMEM((4, 28, B, C), F32),
        ],
        compiler_params=params(),
        cost_estimate=pl.CostEstimate(flops=60_000_000, bytes_accessed=800_000, transcendentals=0),
        name="back",
    )(
        odd,
        even,
        source,
        taps,
        grad_conv,
        branch,
        fluid,
        *weights,
        held[-1],
        *[pinned(array) for array in (up, feat)],
    )

    factor = 1.0 / math.sqrt(parts * B**3)
    summed = pl.pallas_call(
        functools.partial(reduce_kernel, parts, factor),
        out_shape=jax.ShapeDtypeStruct((parts, chunk, LANES), BF16),
        in_specs=[vmem(), pl.BlockSpec(memory_space=pl.ANY)],
        out_specs=vmem(),
        compiler_params=params(),
        name="reduce",
    )(scattered, pinned(grad_field))
    gathered = lax.all_to_all(summed, axes, 0, 0, tiled=True)
    grad_kernel, grad_w_in, grad_w_out, grad_b_in, grad_vectors = pl.pallas_call(
        functools.partial(unpack_kernel, chunk),
        out_shape=[
            jax.ShapeDtypeStruct((T, T, T, C), F32),
            jax.ShapeDtypeStruct((C, HID), F32),
            jax.ShapeDtypeStruct((C, HID), F32),
            jax.ShapeDtypeStruct((HID,), F32),
            jax.ShapeDtypeStruct((4, C), F32),
        ],
        in_specs=[vmem()],
        out_specs=[vmem()] * 5,
        scratch_shapes=[pltpu.VMEM((ROWS, LANES), F32)],
        compiler_params=params(),
        name="unpack",
    )(gathered)
    lead = (1, 1, 1)
    return (
        mixed.reshape(lead + block),
        grad_field.reshape(lead + block),
        grad_kernel,
        grad_w_in,
        grad_w_out.T,
        grad_b_in,
        grad_vectors,
    )


def solution(mesh):
    return jax.shard_map(
        local,
        mesh=mesh,
        in_specs=(
            P("sample", "space", None, None, None, None),
            P("sample", "space", None, None, None),
            P("sample", None, None),
            P(),
            P(),
            P(),
            P(),
            P(),
            P(),
            P(),
            P(),
            P("sample", "space", None, None, None, None),
        ),
        out_specs=(
            P("sample", "space", None, None, None, None),
            P("sample", "space", None, None, None, None),
            P(),
            P(),
            P(),
            P(),
            P(),
        ),
        check_vma=False,
    )
```
